32 devices in a mesh: gx: 4 (over y, core), gy: 4 (over z), gz: 2 (over x).
Axes of the slice: x: 2, y: 2, z: 4, core: 2. Of those that a mesh axis runs over, the one named last changes fastest.
Arguments:
- inputs: bfloat16 [64, 16, 32, 256], P(None, 'gx', 'gy', 'gz'), may hold values from -6 to 6
- weight: bfloat16 [4, 4, 4, 64, 32], replicated, may hold values from -0.25 to 0.25
- cotangent: bfloat16 [2, 2, 2, 32, 16, 32, 256], P(None, None, None, None, 'gx', 'gy', 'gz'), may hold values from -3 to 3
Outputs:
- upsampled: bfloat16 [2, 2, 2, 32, 16, 32, 256], P(None, None, None, None, 'gx', 'gy', 'gz')
- input_grad: bfloat16 [64, 16, 32, 256], P(None, 'gx', 'gy', 'gz')
- weight_grad: float32 [4, 4, 4, 64, 32], replicated
The draws below stay inside these ranges and needn't reach their ends.
All inputs are finite; a program needn't handle non-finite values.
Results may differ from the reference program's by a relative error of at most 0.0018.
Values may be sent and summed in bfloat16 or wider, within the bound.
A program may use at most 192 MiB of HBM per device.

```python
import math
import jax
import jax.numpy as jnp
from jax import lax

CIN = 64
COUT = 32
K = 4
NX = 16
NY = 32
NZ = 256


def level_of(rng, shape, pieces, smallest, high):
    factor_of, own = 1.0, jax.random.fold_in(rng, 6)
    for dim, blocks in pieces:
        steps = jnp.exp(jax.random.uniform(jax.random.fold_in(own, dim), (blocks,), jnp.float32, smallest / len(pieces), high / len(pieces)))
        factor_of = factor_of * jnp.repeat(steps, shape[dim] // blocks).reshape([-1 if axis == dim else 1 for axis in range(len(shape))])
    return factor_of


def scatter_about(rng, extent, scale, bound, pieces=(), kind=jnp.bfloat16):
    values = scale * jax.random.normal(rng, extent, jnp.float32)
    if pieces:
        values = values * level_of(rng, extent, pieces, -0.22, 0.18)
    return jnp.clip(values, -bound, bound).astype(kind)


def setup_inputs(seed: int = 0) -> dict:
    key_list = jax.random.split(jax.random.key(seed), 4)
    return {
        "inputs": scatter_about(key_list[0], (CIN, NX, NY, NZ), 1.0, 6.0, ((1, 4), (2, 4), (3, 2))),
        "weight": scatter_about(key_list[1], (K, K, K, CIN, COUT), (8 * CIN) ** -0.5, 0.25),
        "cotangent": scatter_about(key_list[2], (2, 2, 2, COUT, NX, NY, NZ), 0.5, 3.0, ((4, 4), (5, 4), (6, 2))),
    }


def transposed(inputs_wide, weight_wide):
    padded = jnp.pad(inputs_wide, ((0, 0), (1, 1), (1, 1), (0, 0)), mode='wrap')
    kernel = jnp.transpose(jnp.flip(weight_wide, (0, 1, 2)), (4, 3, 0, 1, 2))
    result = lax.conv_general_dilated(padded[None], kernel, (1, 1, 1), ((0, 0), (0, 0), (2, 2)), lhs_dilation=(2, 2, 2), dimension_numbers=('NCDHW', 'OIDHW', 'NCDHW'), precision=lax.Precision.HIGHEST)
    return result[0]

def to_subpixel(full):
    channels = full.shape[0]
    split = full.reshape((channels, NX, 2, NY, 2, NZ, 2))
    return split.transpose(2, 4, 6, 0, 1, 3, 5)

def from_subpixel(packed):
    channels = packed.shape[3]
    moved = packed.transpose(3, 4, 0, 5, 1, 6, 2)
    return moved.reshape((channels, 2 * NX, 2 * NY, 2 * NZ))

def reference(inputs, weight, cotangent):
    inputs_wide = inputs.astype(jnp.float32)
    weight_wide = weight.astype(jnp.float32)
    result, pullback = jax.vjp(transposed, inputs_wide, weight_wide)
    input_grad, weight_grad = pullback(from_subpixel(cotangent.astype(jnp.float32)))
    factor = 1.0 / math.sqrt(NX * NY * NZ)
    return (to_subpixel(result).astype(jnp.bfloat16), input_grad.astype(jnp.bfloat16), weight_grad * factor)
```

```python
import functools
import math

import jax
import jax.numpy as jnp
from jax import lax
from jax.experimental import pallas as pl
from jax.experimental.pallas import tpu as pltpu
from jax.sharding import PartitionSpec as P

TAPS = ((1, 3), (2, 0))
G_OFF = ((0, 1), (1, 0))
IN_SHIFT = ((0, -1), (0, 1))
PAIRS = [(p, h) for p in (0, 1) for h in (0, 1)]


def ring(value, axis, step):
    count = lax.axis_size(axis)
    return lax.ppermute(value, axis, [(i, (i + step) % count) for i in range(count)])


def line(value, axis, step):
    count = lax.axis_size(axis)
    pairs = [(i, i + step) for i in range(count) if 0 <= i + step < count]
    return lax.ppermute(value, axis, pairs)


def reorder(weight):
    for dim in range(3):
        parts = [lax.slice_in_dim(weight, k, k + 1, axis=dim) for k in (1, 3, 2, 0)]
        weight = jnp.concatenate(parts, axis=dim)
    return weight


def inverse_order(taps):
    for dim in range(3):
        parts = [lax.slice_in_dim(taps, k, k + 1, axis=dim) for k in (3, 0, 2, 1)]
        taps = jnp.concatenate(parts, axis=dim)
    return taps


def dot(a, b):
    return jnp.dot(a, b, preferred_element_type=jnp.float32)


def dot_nt(a, b):
    return lax.dot_general(a, b, (((1,), (1,)), ((), ())), preferred_element_type=jnp.float32)


def compute_kernel(in_ref, g_ref, zin_ref, zg_ref, wf_ref, wi_ref, up_ref, ig_ref, wg_ref):
    cells_x, cells_y, _, cells_z = ig_ref.shape
    in_ch = ig_ref.shape[2]
    out_ch = up_ref.shape[3] // 2
    wide = zin_ref.shape[-1]
    lane = lax.broadcasted_iota(jnp.int32, (in_ch, cells_z), 1)
    first = lane == 0
    last = lane == cells_z - 1

    def rolled(value, amount):
        return pltpu.roll(value, amount % value.shape[-1], 1)

    edge_up = []
    for px in (0, 1):
        for py in (0, 1):
            halves = []
            for pz in (0, 1):
                packed = zin_ref[pz].astype(jnp.float32)
                rows = []
                for hx in (0, 1):
                    for hy in (0, 1):
                        spot = (1 + IN_SHIFT[px][hx]) * (cells_y + 2) + 1 + IN_SHIFT[py][hy]
                        rows.append(rolled(packed, -spot))
                stacked = jnp.concatenate(rows, axis=0).astype(jnp.bfloat16)
                halves.append(
                    dot(wf_ref[px * 2 + py, pl.ds((2 * pz + 1) * out_ch, out_ch), :], stacked)
                )
            edge_up.append(halves)
    edge_ig = []
    for pz in (0, 1):
        rows = []
        for px, hx in PAIRS:
            for py, hy in PAIRS:
                packed = zg_ref[pz, px * 2 + py].astype(jnp.float32)
                spot = G_OFF[px][hx] * (cells_y + 1) + G_OFF[py][hy]
                rows.append(rolled(packed, -spot))
        stacked = jnp.concatenate(rows, axis=0).astype(jnp.bfloat16)
        edge_ig.append(dot(wi_ref[pz, in_ch : 2 * in_ch, :], stacked))

    wg_ref[...] = jnp.zeros_like(wg_ref)
    for x in range(cells_x):
        parts = [[], []]
        for pz in (0, 1):
            rows = []
            for px, hx in PAIRS:
                for py, hy in PAIRS:
                    rows.append(
                        jnp.concatenate(
                            [
                                g_ref[
                                    x + G_OFF[px][hx],
                                    y + G_OFF[py][hy],
                                    px * 2 + py,
                                    pl.ds(pz * out_ch, out_ch),
                                    :,
                                ]
                                for y in range(cells_y)
                            ],
                            axis=1,
                        )
                    )
            grads = jnp.concatenate(rows, axis=0)
            product = dot(wi_ref[pz], grads)
            shifted = []
            for y in range(cells_y):
                cols = slice(y * cells_z, (y + 1) * cells_z)
                spot = x * (cells_y + 1) + y
                if pz == 0:
                    far = rolled(product[in_ch:, cols], -1)
                    edge = rolled(edge_ig[0], cells_z - 1 - spot)
                    far = jnp.where(last, edge, far)
                else:
                    far = rolled(product[in_ch:, cols], 1)
                    edge = rolled(edge_ig[1], -spot)
                    far = jnp.where(first, edge, far)
                parts[pz].append(product[:in_ch, cols] + far)
                here = in_ref[x + 1, y + 1]
                packed = zin_ref[pz].astype(jnp.float32)
                spot = (x + 1) * (cells_y + 2) + y + 1
                if pz == 0:
                    near = jnp.where(
                        first, rolled(packed, -spot), rolled(here.astype(jnp.float32), 1)
                    )
                else:
                    near = jnp.where(
                        last,
                        rolled(packed, cells_z - 1 - spot),
                        rolled(here.astype(jnp.float32), -1),
                    )
                shifted.append(jnp.concatenate([here, near.astype(jnp.bfloat16)], axis=0))
            wg_ref[pz] += dot_nt(grads, jnp.concatenate(shifted, axis=1))
        for y in range(cells_y):
            ig_ref[x, y] = (parts[0][y] + parts[1][y]).astype(jnp.bfloat16)
        for px in (0, 1):
            for py in (0, 1):
                rows = []
                for hx in (0, 1):
                    for hy in (0, 1):
                        rows.append(
                            jnp.concatenate(
                                [
                                    in_ref[
                                        x + 1 + IN_SHIFT[px][hx], y + 1 + IN_SHIFT[py][hy]
                                    ]
                                    for y in range(cells_y)
                                ],
                                axis=1,
                            )
                        )
                product = dot(wf_ref[px * 2 + py], jnp.concatenate(rows, axis=0))
                for y in range(cells_y):
                    cols = slice(y * cells_z, (y + 1) * cells_z)
                    spot = x * (cells_y + 2) + y
                    edge0, edge1 = edge_up[px * 2 + py]
                    even = product[:out_ch, cols] + jnp.where(
                        first[:out_ch],
                        rolled(edge0, -spot),
                        rolled(product[out_ch : 2 * out_ch, cols], 1),
                    )
                    odd = product[2 * out_ch : 3 * out_ch, cols] + jnp.where(
                        last[:out_ch],
                        rolled(edge1, cells_z - 1 - spot),
                        rolled(product[3 * out_ch :, cols], -1),
                    )
                    up_ref[x, y, px * 2 + py, :out_ch] = even.astype(jnp.bfloat16)
                    up_ref[x, y, px * 2 + py, out_ch:] = odd.astype(jnp.bfloat16)


def packed_lanes(columns):
    count = columns.shape[0] * columns.shape[1]
    flat = jnp.moveaxis(columns.reshape((count,) + columns.shape[2:]), 0, -1)
    return jnp.pad(flat, [(0, 0)] * (flat.ndim - 1) + [(0, 128 - count)])


def body(inputs, weight, cotangent):
    in_ch, cells_x, cells_y, cells_z = inputs.shape
    out_ch = weight.shape[4]
    cells = inputs.transpose(1, 2, 0, 3)
    cells = jnp.concatenate([ring(cells[-1:], "gx", 1), cells, ring(cells[:1], "gx", -1)], axis=0)
    cells = jnp.concatenate(
        [ring(cells[:, -1:], "gy", 1), cells, ring(cells[:, :1], "gy", -1)], axis=1
    )
    grads = cotangent.transpose(4, 5, 0, 1, 2, 3, 6).reshape(
        (cells_x, cells_y, 2, 2, 2 * out_ch, cells_z)
    )
    grads = jnp.concatenate(
        [
            jnp.concatenate([grads[:, :, :1], ring(grads[:1, :, :1], "gx", -1)], axis=0),
            jnp.concatenate([ring(grads[-1:, :, 1:], "gx", 1), grads[:, :, 1:]], axis=0),
        ],
        axis=2,
    )
    grads = jnp.concatenate(
        [
            jnp.concatenate([grads[..., :1, :, :], ring(grads[:, :1, :, :1], "gy", -1)], axis=1),
            jnp.concatenate([ring(grads[:, -1:, :, 1:], "gy", 1), grads[..., 1:, :, :]], axis=1),
        ],
        axis=3,
    ).reshape((cells_x + 1, cells_y + 1, 4, 2 * out_ch, cells_z))
    z_in = jnp.stack(
        [
            line(packed_lanes(cells[..., -1]), "gz", 1),
            line(packed_lanes(cells[..., 0]), "gz", -1),
        ]
    )
    z_g = jnp.stack(
        [
            line(packed_lanes(grads[:, :, :, :out_ch, 0]), "gz", -1),
            line(packed_lanes(grads[:, :, :, out_ch:, -1]), "gz", 1),
        ]
    )
    taps = reorder(weight).reshape((2, 2, 2, 2, 2, 2, in_ch, out_ch))
    w_f = taps.transpose(0, 2, 4, 5, 7, 1, 3, 6).reshape((4, 4 * out_ch, 4 * in_ch))
    w_i = taps.transpose(4, 5, 6, 0, 1, 2, 3, 7).reshape((2, 2 * in_ch, 16 * out_ch))
    up, ig, wg = pl.pallas_call(
        compute_kernel,
        out_shape=(
            jax.ShapeDtypeStruct((cells_x, cells_y, 4, 2 * out_ch, cells_z), jnp.bfloat16),
            jax.ShapeDtypeStruct((cells_x, cells_y, in_ch, cells_z), jnp.bfloat16),
            jax.ShapeDtypeStruct((2, 16 * out_ch, 2 * in_ch), jnp.float32),
        ),
        in_specs=[pl.BlockSpec(memory_space=pltpu.VMEM)] * 6,
        out_specs=[pl.BlockSpec(memory_space=pltpu.VMEM)] * 3,
        compiler_params=pltpu.CompilerParams(vmem_limit_bytes=48 * 1024 * 1024),
    )(cells, grads, z_in, z_g, w_f, w_i)
    up = up.reshape((cells_x, cells_y, 2, 2, 2, out_ch, cells_z)).transpose(2, 3, 4, 5, 0, 1, 6)
    ig = ig.transpose(2, 0, 1, 3)
    total = lax.psum(wg, ("gx", "gy", "gz"))
    total = total.reshape((2, 2, 2, 2, 2, out_ch, 2, in_ch)).transpose(1, 2, 3, 4, 0, 6, 7, 5)
    total = inverse_order(total.reshape((4, 4, 4, in_ch, out_ch)))
    all_cells = (
        cells_x
        * lax.axis_size("gx")
        * cells_y
        * lax.axis_size("gy")
        * cells_z
        * lax.axis_size("gz")
    )
    return up, ig, total * (1.0 / math.sqrt(all_cells))


def solution(mesh):
    placed = (P(None, "gx", "gy", "gz"), P(), P(None, None, None, None, "gx", "gy", "gz"))
    return jax.shard_map(
        body,
        mesh=mesh,
        in_specs=placed,
        out_specs=(P(None, None, None, None, "gx", "gy", "gz"), P(None, "gx", "gy", "gz"), P()),
        check_vma=False,
    )
```

```python
import functools
import math

import jax
import jax.numpy as jnp
from jax import lax
from jax.experimental import pallas as pl
from jax.experimental.pallas import tpu as pltpu
from jax.sharding import PartitionSpec as P

TAPS = ((1, 3), (2, 0))
G_OFF = ((0, 1), (1, 0))
IN_SHIFT = ((0, -1), (0, 1))
PAIRS = [(p, h) for p in (0, 1) for h in (0, 1)]


MESH = pl.DeviceIdType.MESH


def dot(a, b):
    return jnp.dot(a, b, preferred_element_type=jnp.float32)


def dot_nt(a, b):
    return lax.dot_general(a, b, (((1,), (1,)), ((), ())), preferred_element_type=jnp.float32)


def compute_kernel(
    in_ref, g_ref, zin_ref, zg_ref, w_ref, up_ref, ig_ref, wg_ref, wf_ref, wi_ref
):
    cells_x, cells_y, _, cells_z = ig_ref.shape
    in_ch = ig_ref.shape[2]
    out_ch = up_ref.shape[3] // 2
    wide = zin_ref.shape[-1]
    lane = lax.broadcasted_iota(jnp.int32, (in_ch, cells_z), 1)
    first = lane == 0
    last = lane == cells_z - 1

    def rolled(value, amount):
        return pltpu.roll(value, amount % value.shape[-1], 1)

    for px in (0, 1):
        for py in (0, 1):
            for pz, hz in PAIRS:
                wf_ref[px * 2 + py, pl.ds((2 * pz + hz) * out_ch, out_ch), :] = jnp.concatenate(
                    [
                        w_ref[TAPS[px][hx], TAPS[py][hy], TAPS[pz][hz]]
                        for hx in (0, 1)
                        for hy in (0, 1)
                    ],
                    axis=1,
                )
    for pz in (0, 1):
        rows = [
            jnp.concatenate(
                [w_ref[TAPS[px][hx], TAPS[py][hy], TAPS[pz][hz]] for hz in (0, 1)], axis=1
            )
            for px, hx in PAIRS
            for py, hy in PAIRS
        ]
        stacked = jnp.concatenate(rows, axis=0).astype(jnp.float32)
        wi_ref[pz] = stacked.T.astype(jnp.bfloat16)

    edge_up = []
    for px in (0, 1):
        for py in (0, 1):
            halves = []
            for pz in (0, 1):
                packed = zin_ref[pz].astype(jnp.float32)
                rows = []
                for hx in (0, 1):
                    for hy in (0, 1):
                        spot = (1 + IN_SHIFT[px][hx]) * (cells_y + 2) + 1 + IN_SHIFT[py][hy]
                        rows.append(rolled(packed, -spot))
                stacked = jnp.concatenate(rows, axis=0).astype(jnp.bfloat16)
                halves.append(
                    dot(wf_ref[px * 2 + py, pl.ds((2 * pz + 1) * out_ch, out_ch), :], stacked)
                )
            edge_up.append(halves)
    edge_ig = []
    for pz in (0, 1):
        rows = []
        for px, hx in PAIRS:
            for py, hy in PAIRS:
                packed = zg_ref[pz, px * 2 + py].astype(jnp.float32)
                spot = G_OFF[px][hx] * (cells_y + 1) + G_OFF[py][hy]
                rows.append(rolled(packed, -spot))
        stacked = jnp.concatenate(rows, axis=0).astype(jnp.bfloat16)
        edge_ig.append(dot(wi_ref[pz, in_ch : 2 * in_ch, :], stacked))

    wg_ref[...] = jnp.zeros_like(wg_ref)
    for x in range(cells_x):
        parts = [[], []]
        for pz in (0, 1):
            rows = []
            for px, hx in PAIRS:
                for py, hy in PAIRS:
                    rows.append(
                        jnp.concatenate(
                            [
                                g_ref[
                                    x + G_OFF[px][hx],
                                    y + G_OFF[py][hy],
                                    px * 2 + py,
                                    pl.ds(pz * out_ch, out_ch),
                                    :,
                                ]
                                for y in range(cells_y)
                            ],
                            axis=1,
                        )
                    )
            grads = jnp.concatenate(rows, axis=0)
            product = dot(wi_ref[pz], grads)
            shifted = []
            for y in range(cells_y):
                cols = slice(y * cells_z, (y + 1) * cells_z)
                spot = x * (cells_y + 1) + y
                if pz == 0:
                    far = rolled(product[in_ch:, cols], -1)
                    edge = rolled(edge_ig[0], cells_z - 1 - spot)
                    far = jnp.where(last, edge, far)
                else:
                    far = rolled(product[in_ch:, cols], 1)
                    edge = rolled(edge_ig[1], -spot)
                    far = jnp.where(first, edge, far)
                parts[pz].append(product[:in_ch, cols] + far)
                here = in_ref[x + 1, y + 1]
                packed = zin_ref[pz].astype(jnp.float32)
                spot = (x + 1) * (cells_y + 2) + y + 1
                if pz == 0:
                    near = jnp.where(
                        first, rolled(packed, -spot), rolled(here.astype(jnp.float32), 1)
                    )
                else:
                    near = jnp.where(
                        last,
                        rolled(packed, cells_z - 1 - spot),
                        rolled(here.astype(jnp.float32), -1),
                    )
                shifted.append(jnp.concatenate([here, near.astype(jnp.bfloat16)], axis=0))
            wg_ref[pz] += dot_nt(grads, jnp.concatenate(shifted, axis=1))
        for y in range(cells_y):
            ig_ref[x, y] = (parts[0][y] + parts[1][y]).astype(jnp.bfloat16)
        for px in (0, 1):
            for py in (0, 1):
                rows = []
                for hx in (0, 1):
                    for hy in (0, 1):
                        rows.append(
                            jnp.concatenate(
                                [
                                    in_ref[
                                        x + 1 + IN_SHIFT[px][hx], y + 1 + IN_SHIFT[py][hy]
                                    ]
                                    for y in range(cells_y)
                                ],
                                axis=1,
                            )
                        )
                product = dot(wf_ref[px * 2 + py], jnp.concatenate(rows, axis=0))
                for y in range(cells_y):
                    cols = slice(y * cells_z, (y + 1) * cells_z)
                    spot = x * (cells_y + 2) + y
                    edge0, edge1 = edge_up[px * 2 + py]
                    even = product[:out_ch, cols] + jnp.where(
                        first[:out_ch],
                        rolled(edge0, -spot),
                        rolled(product[out_ch : 2 * out_ch, cols], 1),
                    )
                    odd = product[2 * out_ch : 3 * out_ch, cols] + jnp.where(
                        last[:out_ch],
                        rolled(edge1, cells_z - 1 - spot),
                        rolled(product[3 * out_ch :, cols], -1),
                    )
                    up_ref[x, y, px * 2 + py, :out_ch] = even.astype(jnp.bfloat16)
                    up_ref[x, y, px * 2 + py, out_ch:] = odd.astype(jnp.bfloat16)


def halo_kernel(
    in_ref,
    g_ref,
    ext_ref,
    gext_ref,
    zin_ref,
    zg_ref,
    pack_in,
    pack_g,
    face_in,
    face_g,
    send_sem,
    recv_sem,
):
    cells_x, cells_y, in_ch, cells_z = in_ref.shape
    out_ch = g_ref.shape[3] // 2
    count_x, count_y = lax.axis_size("gx"), lax.axis_size("gy")
    me_x, me_y, me_z = lax.axis_index("gx"), lax.axis_index("gy"), lax.axis_index("gz")
    right_x = {"gx": lax.rem(me_x + 1, count_x)}
    left_x = {"gx": lax.rem(me_x + count_x - 1, count_x)}
    right_y = {"gy": lax.rem(me_y + 1, count_y)}
    left_y = {"gy": lax.rem(me_y + count_y - 1, count_y)}
    other_z = {"gz": 1 - me_z}
    barrier = pltpu.get_barrier_semaphore()
    for neighbour in (right_x, left_x, right_y, left_y, other_z):
        pl.semaphore_signal(barrier, inc=1, device_id=neighbour, device_id_type=MESH)
    pl.semaphore_wait(barrier, 5)

    used = [0]

    def send(src, dst, device):
        n = used[0]
        used[0] += 1
        copy = pltpu.make_async_remote_copy(
            src_ref=src,
            dst_ref=dst,
            send_sem=send_sem.at[n],
            recv_sem=recv_sem.at[n],
            device_id=device,
            device_id_type=MESH,
        )
        copy.start()
        return copy

    inner_x, inner_y = pl.ds(1, cells_x), pl.ds(1, cells_y)
    over_x = [
        send(in_ref.at[cells_x - 1], ext_ref.at[0, inner_y], right_x),
        send(in_ref.at[0], ext_ref.at[cells_x + 1, inner_y], left_x),
    ]
    over_y = [
        send(in_ref.at[:, cells_y - 1], ext_ref.at[inner_x, 0], right_y),
        send(in_ref.at[:, 0], ext_ref.at[inner_x, cells_y + 1], left_y),
    ]
    for px in (0, 1):
        for py in (0, 1):
            n = px * 2 + py
            own_x, own_y = pl.ds(px, cells_x), pl.ds(py, cells_y)
            if px == 0:
                over_x.append(send(g_ref.at[0, :, n], gext_ref.at[cells_x, own_y, n], left_x))
            else:
                over_x.append(send(g_ref.at[cells_x - 1, :, n], gext_ref.at[0, own_y, n], right_x))
            if py == 0:
                over_y.append(send(g_ref.at[:, 0, n], gext_ref.at[own_x, cells_y, n], left_y))
            else:
                over_y.append(send(g_ref.at[:, cells_y - 1, n], gext_ref.at[own_x, 0, n], right_y))

    ext_ref[1 : cells_x + 1, 1 : cells_y + 1] = in_ref[...]
    for px in (0, 1):
        for py in (0, 1):
            n = px * 2 + py
            gext_ref[px : px + cells_x, py : py + cells_y, n] = g_ref[:, :, n]
    zin_ref[me_z] = jnp.zeros_like(zin_ref[0])
    zg_ref[1 - me_z] = jnp.zeros_like(zg_ref[0])

    wide = zin_ref.shape[-1]
    source = (1 - me_z) * (cells_z - 1)
    half = pl.ds(pl.multiple_of((1 - me_z) * out_ch, out_ch), out_ch)

    def pack(dst, load, spot_of, count, stride):
        lane = lax.broadcasted_iota(jnp.int32, dst.shape, 1)

        def step(i, held):
            x, y = spot_of(i)
            spot = x * stride + y
            value = load(x, y).astype(jnp.float32)
            turned = pltpu.roll(value, lax.rem(spot + wide - source, wide), 1)
            return jnp.where(lane == spot, turned, held)

        dst[...] = lax.fori_loop(0, count, step, dst[...])

    def load_in(x, y):
        return ext_ref[x, y]

    def load_g(x, y):
        return gext_ref[x, y, :, half, :].reshape((4 * out_ch, cells_z))

    pack_in[...] = jnp.zeros_like(pack_in)
    pack_g[...] = jnp.zeros_like(pack_g)
    row = cells_y + 2
    pack(pack_in, load_in, lambda i: (1 + i // cells_y, 1 + i % cells_y), cells_x * cells_y, row)
    pack(
        pack_g,
        load_g,
        lambda i: (1 + i // (cells_y - 1), 1 + i % (cells_y - 1)),
        (cells_x - 1) * (cells_y - 1),
        row - 1,
    )

    for copy in over_x:
        copy.wait()
    corners = [
        send(ext_ref.at[0, cells_y], ext_ref.at[0, 0], right_y),
        send(ext_ref.at[cells_x + 1, cells_y], ext_ref.at[cells_x + 1, 0], right_y),
        send(ext_ref.at[0, 1], ext_ref.at[0, cells_y + 1], left_y),
        send(ext_ref.at[cells_x + 1, 1], ext_ref.at[cells_x + 1, cells_y + 1], left_y),
    ]
    for px in (0, 1):
        far = cells_x if px == 0 else 0
        n = px * 2
        corners.append(send(gext_ref.at[far, 0, n], gext_ref.at[far, cells_y, n], left_y))
        corners.append(send(gext_ref.at[far, cells_y, n + 1], gext_ref.at[far, 0, n + 1], right_y))
    for copy in over_y:
        copy.wait()
    pack(
        pack_in,
        load_in,
        lambda i: (1 + i // 2, (i % 2) * (cells_y + 1)),
        2 * cells_x,
        row,
    )
    pack(
        pack_g,
        load_g,
        lambda i: (1 + i // 2, (i % 2) * cells_y),
        2 * (cells_x - 1),
        row - 1,
    )
    for copy in corners:
        copy.wait()
    pack(
        pack_in,
        load_in,
        lambda i: ((i % 2) * (cells_x + 1), i // 2),
        2 * (cells_y + 2),
        row,
    )
    pack(
        pack_g,
        load_g,
        lambda i: ((i % 2) * cells_x, i // 2),
        2 * (cells_y + 1),
        row - 1,
    )
    face_in[...] = pack_in[...].astype(jnp.bfloat16)
    face_g[...] = pack_g[...].astype(jnp.bfloat16)
    over_z = [
        send(face_in, zin_ref.at[me_z], other_z),
        send(face_g, zg_ref.at[1 - me_z], other_z),
    ]
    for copy in over_z:
        copy.wait()


def reduce_kernel(
    streams, factor, part_ref, out_ref, total, landed, gathered, send_sem, recv_sem
):
    rows = part_ref.shape[0]
    each = rows // len(streams)
    steps = len(streams[0])
    place = {}
    for axis, bit in streams[0]:
        me = lax.axis_index(axis)
        side = lax.rem(lax.div(me, bit), 2)
        place[axis, bit] = (side, {axis: me + bit - 2 * bit * side})

    barrier = pltpu.get_barrier_semaphore()
    for side, partner in place.values():
        pl.semaphore_signal(barrier, inc=1, device_id=partner, device_id_type=MESH)
    pl.semaphore_wait(barrier, steps)

    total[...] = part_ref[...]

    def copy(src, dst, n, partner):
        made = pltpu.make_async_remote_copy(
            src_ref=src,
            dst_ref=dst,
            send_sem=send_sem.at[n],
            recv_sem=recv_sem.at[n],
            device_id=partner,
            device_id_type=MESH,
        )
        made.start()
        return made

    starts = [j * each for j in range(len(streams))]
    kept = [[] for _ in streams]
    for step in range(steps):
        size = each >> (step + 1)
        flying = []
        for j, order in enumerate(streams):
            side, partner = place[order[step]]
            keep = pl.multiple_of(starts[j] + side * size, 8)
            give = pl.multiple_of(starts[j] + (1 - side) * size, 8)
            area = pl.ds(j * each + each - 2 * size, size)
            flying.append(
                copy(
                    total.at[pl.ds(give, size)],
                    landed.at[area],
                    j * steps + step,
                    partner,
                )
            )
            starts[j] = keep
            kept[j].append(keep)
        for j in range(len(streams)):
            flying[j].wait()
            area = pl.ds(j * each + each - 2 * size, size)
            mine = pl.ds(starts[j], size)
            total[mine, :] = total[mine, :] + landed[area, :]
    for j in range(len(streams)):
        mine = pl.ds(starts[j], each >> steps)
        gathered[mine, :] = total[mine, :]
    base = len(streams) * steps
    for step in reversed(range(steps)):
        size = each >> (step + 1)
        flying = []
        for j, order in enumerate(streams):
            partner = place[order[step]][1]
            mine = pl.ds(kept[j][step], size)
            flying.append(
                copy(gathered.at[mine], gathered.at[mine], base + j * steps + step, partner)
            )
        for made in flying:
            made.wait()

    out_ch, in_ch = out_ref.shape[3:]
    for pz in (0, 1):
        for a, (px, hx) in enumerate(PAIRS):
            for b, (py, hy) in enumerate(PAIRS):
                block = gathered[pl.ds(((pz * 4 + a) * 4 + b) * out_ch, out_ch), :] * factor
                for hz in (0, 1):
                    out_ref[TAPS[px][hx], TAPS[py][hy], TAPS[pz][hz]] = block[
                        :, hz * in_ch : (hz + 1) * in_ch
                    ]


def reduce_plan(rows):
    sizes = {axis: lax.axis_size(axis) for axis in ("gz", "gx", "gy")}
    rest = [
        (axis, 1 << bit)
        for axis, size in sizes.items()
        for bit in range(size.bit_length() - 1)
        if (axis, bit) != ("gx", 0)
    ]
    devices = math.prod(sizes.values())
    count = max(1, min(len(rest), rows // (8 * devices)))
    streams = [[("gx", 1)] + rest[j:] + rest[:j] for j in range(count)]
    return streams


def body(inputs, weight, cotangent):
    in_ch, cells_x, cells_y, cells_z = inputs.shape
    out_ch = weight.shape[4]
    cells = inputs.transpose(1, 2, 0, 3)
    grads = cotangent.transpose(4, 5, 0, 1, 2, 3, 6).reshape(
        (cells_x, cells_y, 4, 2 * out_ch, cells_z)
    )
    taps = weight.transpose(0, 1, 2, 4, 3)
    vmem = pl.BlockSpec(memory_space=pltpu.VMEM)
    cells, grads, z_in, z_g = pl.pallas_call(
        halo_kernel,
        out_shape=(
            jax.ShapeDtypeStruct((cells_x + 2, cells_y + 2, in_ch, cells_z), jnp.bfloat16),
            jax.ShapeDtypeStruct((cells_x + 1, cells_y + 1, 4, 2 * out_ch, cells_z), jnp.bfloat16),
            jax.ShapeDtypeStruct((2, in_ch, 128), jnp.bfloat16),
            jax.ShapeDtypeStruct((2, 4 * out_ch, 128), jnp.bfloat16),
        ),
        in_specs=[vmem] * 2,
        out_specs=[vmem] * 4,
        scratch_shapes=[
            pltpu.VMEM((in_ch, 128), jnp.float32),
            pltpu.VMEM((4 * out_ch, 128), jnp.float32),
            pltpu.VMEM((in_ch, 128), jnp.bfloat16),
            pltpu.VMEM((4 * out_ch, 128), jnp.bfloat16),
            pltpu.SemaphoreType.DMA((22,)),
            pltpu.SemaphoreType.DMA((22,)),
        ],
        compiler_params=pltpu.CompilerParams(
            collective_id=0, has_side_effects=True, vmem_limit_bytes=48 * 1024 * 1024
        ),
    )(cells, grads)
    up, ig, wg = pl.pallas_call(
        compute_kernel,
        out_shape=(
            jax.ShapeDtypeStruct((cells_x, cells_y, 4, 2 * out_ch, cells_z), jnp.bfloat16),
            jax.ShapeDtypeStruct((cells_x, cells_y, in_ch, cells_z), jnp.bfloat16),
            jax.ShapeDtypeStruct((2, 16 * out_ch, 2 * in_ch), jnp.float32),
        ),
        in_specs=[vmem] * 5,
        out_specs=[vmem] * 3,
        scratch_shapes=[
            pltpu.VMEM((4, 4 * out_ch, 4 * in_ch), jnp.bfloat16),
            pltpu.VMEM((2, 2 * in_ch, 16 * out_ch), jnp.bfloat16),
        ],
        compiler_params=pltpu.CompilerParams(vmem_limit_bytes=48 * 1024 * 1024),
    )(cells, grads, z_in, z_g.reshape((2, 4, out_ch, 128)), taps)
    up = up.reshape((cells_x, cells_y, 2, 2, 2, out_ch, cells_z)).transpose(2, 3, 4, 5, 0, 1, 6)
    ig = ig.transpose(2, 0, 1, 3)
    all_cells = (
        cells_x
        * lax.axis_size("gx")
        * cells_y
        * lax.axis_size("gy")
        * cells_z
        * lax.axis_size("gz")
    )
    rows = 32 * out_ch
    plan = reduce_plan(rows)
    copies = 2 * len(plan) * len(plan[0])
    total = pl.pallas_call(
        functools.partial(reduce_kernel, plan, 1.0 / math.sqrt(all_cells)),
        out_shape=jax.ShapeDtypeStruct((4, 4, 4, out_ch, in_ch), jnp.float32),
        in_specs=[vmem],
        out_specs=vmem,
        scratch_shapes=[
            pltpu.VMEM((rows, 2 * in_ch), jnp.float32),
            pltpu.VMEM((rows, 2 * in_ch), jnp.float32),
            pltpu.VMEM((rows, 2 * in_ch), jnp.float32),
            pltpu.SemaphoreType.DMA((copies,)),
            pltpu.SemaphoreType.DMA((copies,)),
        ],
        compiler_params=pltpu.CompilerParams(
            collective_id=1, has_side_effects=True, vmem_limit_bytes=48 * 1024 * 1024
        ),
    )(wg.reshape((rows, 2 * in_ch)))
    return up, ig, total.transpose(0, 1, 2, 4, 3)


def solution(mesh):
    placed = (P(None, "gx", "gy", "gz"), P(), P(None, None, None, None, "gx", "gy", "gz"))
    return jax.shard_map(
        body,
        mesh=mesh,
        in_specs=placed,
        out_specs=(P(None, None, None, None, "gx", "gy", "gz"), P(None, "gx", "gy", "gz"), P()),
        check_vma=False,
    )
```

```python
import functools
import math

import jax
import jax.numpy as jnp
from jax import lax
from jax.experimental import pallas as pl
from jax.experimental.pallas import tpu as pltpu
from jax.sharding import PartitionSpec as P

TAPS = ((1, 3), (2, 0))
G_OFF = ((0, 1), (1, 0))
IN_SHIFT = ((0, -1), (0, 1))
PAIRS = [(p, h) for p in (0, 1) for h in (0, 1)]


MESH = pl.DeviceIdType.MESH


def dot(a, b):
    return jnp.dot(a, b, preferred_element_type=jnp.float32)


def dot_nt(a, b):
    return lax.dot_general(a, b, (((1,), (1,)), ((), ())), preferred_element_type=jnp.float32)


def fused_kernel(
    streams,
    factor,
    in_ref,
    g_ref,
    w_ref,
    up_ref,
    ig_ref,
    out_ref,
    ext_ref,
    gext_ref,
    zin_ref,
    zg_ref,
    pack_in,
    pack_g,
    face_in,
    face_g,
    wf_ref,
    wi_ref,
    total,
    landed,
    gathered,
    send_sem,
    recv_sem,
):
    cells_x, cells_y, in_ch, cells_z = in_ref.shape
    out_ch = g_ref.shape[3] // 2
    wide = zin_ref.shape[-1]
    row = cells_y + 2
    count_x, count_y = lax.axis_size("gx"), lax.axis_size("gy")
    me_x, me_y, me_z = lax.axis_index("gx"), lax.axis_index("gy"), lax.axis_index("gz")
    to_x = (lax.rem(me_x + count_x - 1, count_x), lax.rem(me_x + 1, count_x))
    to_y = (lax.rem(me_y + count_y - 1, count_y), lax.rem(me_y + 1, count_y))
    other_z = {"gz": 1 - me_z}

    groups = {}
    for stage in streams[0]:
        sides = [lax.rem(lax.div(lax.axis_index(axis), bit), 2) for axis, bit in stage]
        own = sum(side << i for i, side in enumerate(sides))
        partners = []
        for change in range(1, 1 << len(stage)):
            device, number = {}, own
            for i, (axis, bit) in enumerate(stage):
                if (change >> i) % 2:
                    step = 1 - 2 * sides[i]
                    device[axis] = device.get(axis, lax.axis_index(axis)) + bit * step
                    number = number + (step << i)
            partners.append((device, number))
        groups[stage] = (own, partners)

    greeted = [{"gx": x} for x in to_x] + [{"gy": y} for y in to_y]
    greeted += [{"gx": x, "gy": y} for x in to_x for y in to_y] + [other_z]
    greeted += [device for _, partners in groups.values() for device, _ in partners]
    barrier = pltpu.get_barrier_semaphore()
    for device in greeted:
        pl.semaphore_signal(barrier, inc=1, device_id=device, device_id_type=MESH)
    pl.semaphore_wait(barrier, len(greeted))

    used = [0]

    def send(src, dst, device):
        n = used[0]
        used[0] += 1
        copy = pltpu.make_async_remote_copy(
            src_ref=src,
            dst_ref=dst,
            send_sem=send_sem.at[n],
            recv_sem=recv_sem.at[n],
            device_id=device,
            device_id_type=MESH,
        )
        copy.start()
        return copy

    inner_x, inner_y = pl.ds(1, cells_x), pl.ds(1, cells_y)
    edge_x, edge_y = (0, cells_x - 1), (0, cells_y - 1)
    spot_x, spot_y = (cells_x + 1, 0), (cells_y + 1, 0)
    over_in, over_g = [], []
    for i in (0, 1):
        over_in.append(
            send(in_ref.at[edge_x[i]], ext_ref.at[spot_x[i], inner_y], {"gx": to_x[i]})
        )
        over_in.append(
            send(in_ref.at[:, edge_y[i]], ext_ref.at[inner_x, spot_y[i]], {"gy": to_y[i]})
        )
        for j in (0, 1):
            over_in.append(
                send(
                    in_ref.at[edge_x[i], edge_y[j]],
                    ext_ref.at[spot_x[i], spot_y[j]],
                    {"gx": to_x[i], "gy": to_y[j]},
                )
            )
    far_x, far_y = (cells_x, 0), (cells_y, 0)
    for px in (0, 1):
        for py in (0, 1):
            n = px * 2 + py
            own_x, own_y = pl.ds(px, cells_x), pl.ds(py, cells_y)
            over_g.append(
                send(
                    g_ref.at[edge_x[px], :, n],
                    gext_ref.at[far_x[px], own_y, n],
                    {"gx": to_x[px]},
                )
            )
            over_g.append(
                send(
                    g_ref.at[:, edge_y[py], n],
                    gext_ref.at[own_x, far_y[py], n],
                    {"gy": to_y[py]},
                )
            )
            over_g.append(
                send(
                    g_ref.at[edge_x[px], edge_y[py], n],
                    gext_ref.at[far_x[px], far_y[py], n],
                    {"gx": to_x[px], "gy": to_y[py]},
                )
            )

    ext_ref[1 : cells_x + 1, 1 : cells_y + 1] = in_ref[...]
    for px in (0, 1):
        for py in (0, 1):
            n = px * 2 + py
            gext_ref[px : px + cells_x, py : py + cells_y, n] = g_ref[:, :, n]
    zin_ref[me_z] = jnp.zeros_like(zin_ref[0])
    zg_ref[1 - me_z] = jnp.zeros_like(zg_ref[0])

    source = (1 - me_z) * (cells_z - 1)
    half = pl.ds(pl.multiple_of((1 - me_z) * out_ch, out_ch), out_ch)

    def pack(dst, load, spots, stride):
        lane = lax.broadcasted_iota(jnp.int32, dst.shape, 1)
        held = dst[...]
        for x, y in spots:
            spot = x * stride + y
            value = load(x, y).astype(jnp.float32)
            turned = pltpu.roll(value, lax.rem(spot + wide - source, wide), 1)
            held = jnp.where(lane == spot, turned, held)
        dst[...] = held

    def load_in(x, y):
        return ext_ref[x, y]

    def load_g(x, y):
        return gext_ref[x, y, :, half, :].reshape((4 * out_ch, cells_z))

    inside = [(x, y) for x in range(1, cells_x + 1) for y in range(1, cells_y + 1)]
    around = [
        (x, y) for x in range(cells_x + 2) for y in range(cells_y + 2) if (x, y) not in inside
    ]
    inside_g = [(x, y) for x in range(1, cells_x) for y in range(1, cells_y)]
    around_g = [
        (x, y) for x in range(cells_x + 1) for y in range(cells_y + 1) if (x, y) not in inside_g
    ]
    pack_in[...] = jnp.zeros_like(pack_in)
    pack_g[...] = jnp.zeros_like(pack_g)
    pack(pack_in, load_in, inside, row)

    for px in (0, 1):
        for py in (0, 1):
            for pz, hz in PAIRS:
                wf_ref[px * 2 + py, pl.ds((2 * pz + hz) * out_ch, out_ch), :] = jnp.concatenate(
                    [
                        w_ref[TAPS[px][hx], TAPS[py][hy], TAPS[pz][hz]]
                        for hx in (0, 1)
                        for hy in (0, 1)
                    ],
                    axis=1,
                )
    for pz in (0, 1):
        rows = [
            jnp.concatenate(
                [w_ref[TAPS[px][hx], TAPS[py][hy], TAPS[pz][hz]] for hz in (0, 1)], axis=1
            )
            for px, hx in PAIRS
            for py, hy in PAIRS
        ]
        stacked = jnp.concatenate(rows, axis=0).astype(jnp.float32)
        wi_ref[pz] = stacked.T.astype(jnp.bfloat16)
    pack(pack_g, load_g, inside_g, row - 1)

    for copy in over_in:
        copy.wait()
    pack(pack_in, load_in, around, row)
    face_in[...] = pack_in[...].astype(jnp.bfloat16)
    over_z_in = send(face_in, zin_ref.at[me_z], other_z)

    lane = lax.broadcasted_iota(jnp.int32, (in_ch, cells_z), 1)
    first = lane == 0
    last = lane == cells_z - 1

    def rolled(value, amount):
        return pltpu.roll(value, amount % value.shape[-1], 1)

    over_z_in.wait()

    for px in (0, 1):
        for py in (0, 1):
            n = px * 2 + py
            edges = []
            for pz in (0, 1):
                packed = zin_ref[pz].astype(jnp.float32)
                rows = []
                for hx in (0, 1):
                    for hy in (0, 1):
                        spot = (1 + IN_SHIFT[px][hx]) * row + 1 + IN_SHIFT[py][hy]
                        rows.append(rolled(packed, -spot))
                stacked = jnp.concatenate(rows, axis=0).astype(jnp.bfloat16)
                edges.append(dot(wf_ref[n, pl.ds((2 * pz + 1) * out_ch, out_ch), :], stacked))
            for x in range(cells_x):
                rows = []
                for hx in (0, 1):
                    for hy in (0, 1):
                        rows.append(
                            jnp.concatenate(
                                [
                                    ext_ref[x + 1 + IN_SHIFT[px][hx], y + 1 + IN_SHIFT[py][hy]]
                                    for y in range(cells_y)
                                ],
                                axis=1,
                            )
                        )
                product = dot(wf_ref[n], jnp.concatenate(rows, axis=0))
                for y in range(cells_y):
                    cols = slice(y * cells_z, (y + 1) * cells_z)
                    spot = x * row + y
                    even = product[:out_ch, cols] + jnp.where(
                        first[:out_ch],
                        rolled(edges[0], -spot),
                        rolled(product[out_ch : 2 * out_ch, cols], 1),
                    )
                    odd = product[2 * out_ch : 3 * out_ch, cols] + jnp.where(
                        last[:out_ch],
                        rolled(edges[1], cells_z - 1 - spot),
                        rolled(product[3 * out_ch :, cols], -1),
                    )
                    up_ref[x, y, n, :out_ch] = even.astype(jnp.bfloat16)
                    up_ref[x, y, n, out_ch:] = odd.astype(jnp.bfloat16)

    for copy in over_g:
        copy.wait()
    pack(pack_g, load_g, around_g, row - 1)
    face_g[...] = pack_g[...].astype(jnp.bfloat16)
    over_z_g = send(face_g, zg_ref.at[1 - me_z], other_z)

    def gradients(x, pz):
        rows = []
        for px, hx in PAIRS:
            for py, hy in PAIRS:
                rows.append(
                    jnp.concatenate(
                        [
                            gext_ref[
                                x + G_OFF[px][hx],
                                y + G_OFF[py][hy],
                                px * 2 + py,
                                pl.ds(pz * out_ch, out_ch),
                                :,
                            ]
                            for y in range(cells_y)
                        ],
                        axis=1,
                    )
                )
        return jnp.concatenate(rows, axis=0)

    each = total.shape[0] // len(streams)
    begin = [j * each for j in range(len(streams))]
    length = [each for _ in streams]
    filled = [j * each for j in range(len(streams))]
    kept = [[] for _ in streams]
    flying = [None for _ in streams]

    def scatter(j, stage):
        own, partners = groups[stage]
        size = length[j] // (len(partners) + 1)
        copies = []
        for device, number in partners:
            give = pl.multiple_of(begin[j] + number * size, 8)
            area = pl.ds(filled[j], size)
            filled[j] += size
            copies.append((send(total.at[pl.ds(give, size)], landed.at[area], device), area))
        begin[j] = pl.multiple_of(begin[j] + own * size, 8)
        length[j] = size
        kept[j].append(begin[j])
        flying[j] = copies

    def settle(j):
        mine = pl.ds(begin[j], length[j])
        value = total[mine, :]
        for copy, area in flying[j]:
            copy.wait()
            value = value + landed[area, :]
        total[mine, :] = value

    def gather(j, depth):
        size = length[j]
        mine = pl.ds(kept[j][depth], size)
        flying[j] = [
            send(gathered.at[mine], gathered.at[mine], device)
            for device, _ in groups[streams[j][depth]][1]
        ]
        length[j] = size * (len(flying[j]) + 1)

    def arrive(j):
        for copy in flying[j]:
            copy.wait()

    half_rows = 16 * out_ch
    for pz in (0, 1):
        packed = zin_ref[pz].astype(jnp.float32)
        for x in range(cells_x):
            shifted = []
            for y in range(cells_y):
                here = ext_ref[x + 1, y + 1]
                spot = (x + 1) * row + y + 1
                if pz == 0:
                    near = jnp.where(
                        first, rolled(packed, -spot), rolled(here.astype(jnp.float32), 1)
                    )
                else:
                    near = jnp.where(
                        last,
                        rolled(packed, cells_z - 1 - spot),
                        rolled(here.astype(jnp.float32), -1),
                    )
                shifted.append(jnp.concatenate([here, near.astype(jnp.bfloat16)], axis=0))
            part = dot_nt(gradients(x, pz), jnp.concatenate(shifted, axis=1))
            spots = pl.ds(pz * half_rows, half_rows)
            total[spots, :] = part if x == 0 else total[spots, :] + part
        if len(streams) == 2:
            scatter(pz, streams[pz][0])
    if len(streams) == 1:
        scatter(0, streams[0][0])

    over_z_g.wait()
    edge_ig = []
    for pz in (0, 1):
        rows = []
        for px, hx in PAIRS:
            for py, hy in PAIRS:
                packed = zg_ref[pz, pl.ds((px * 2 + py) * out_ch, out_ch), :].astype(jnp.float32)
                rows.append(rolled(packed, -(G_OFF[px][hx] * (row - 1) + G_OFF[py][hy])))
        stacked = jnp.concatenate(rows, axis=0).astype(jnp.bfloat16)
        edge_ig.append(dot(wi_ref[pz, in_ch : 2 * in_ch, :], stacked))

    def input_row(x):
        parts = [[], []]
        for pz in (0, 1):
            product = dot(wi_ref[pz], gradients(x, pz))
            for y in range(cells_y):
                cols = slice(y * cells_z, (y + 1) * cells_z)
                spot = x * (row - 1) + y
                if pz == 0:
                    far = jnp.where(
                        last,
                        rolled(edge_ig[0], cells_z - 1 - spot),
                        rolled(product[in_ch:, cols], -1),
                    )
                else:
                    far = jnp.where(
                        first, rolled(edge_ig[1], -spot), rolled(product[in_ch:, cols], 1)
                    )
                parts[pz].append(product[:in_ch, cols] + far)
        for y in range(cells_y):
            ig_ref[x, y] = (parts[0][y] + parts[1][y]).astype(jnp.bfloat16)

    left = list(range(cells_x))

    def compute_some():
        if left:
            input_row(left.pop(0))

    stages = len(streams[0])
    everyone = range(len(streams))
    for depth in range(1, stages):
        compute_some()
        for j in everyone:
            settle(j)
            scatter(j, streams[j][depth])
    compute_some()
    for j in everyone:
        settle(j)
        mine = pl.ds(begin[j], length[j])
        gathered[mine, :] = total[mine, :]
        gather(j, stages - 1)
    for depth in reversed(range(stages - 1)):
        compute_some()
        for j in everyone:
            arrive(j)
            gather(j, depth)
    while left:
        compute_some()
    for j in everyone:
        arrive(j)
        for pz in (0, 1):
            if len(streams) == 2 and pz != j:
                continue
            for a, (px, hx) in enumerate(PAIRS):
                for b, (py, hy) in enumerate(PAIRS):
                    spots = pl.ds(((pz * 4 + a) * 4 + b) * out_ch, out_ch)
                    block = gathered[spots, :] * factor
                    for hz in (0, 1):
                        out_ref[TAPS[px][hx], TAPS[py][hy], TAPS[pz][hz]] = block[
                            :, hz * in_ch : (hz + 1) * in_ch
                        ]


def reduce_plan(rows):
    sizes = {axis: lax.axis_size(axis) for axis in ("gz", "gx", "gy")}
    bits = {
        axis: [(axis, 1 << bit) for bit in range(size.bit_length() - 1)]
        for axis, size in sizes.items()
    }
    plane = tuple(bits["gz"] + bits["gx"][1:])
    lines = [tuple(bits["gy"][i : i + 2]) for i in range(0, len(bits["gy"]), 2)]
    core = tuple(bits["gx"][:1])
    streams = [[core, plane] + lines, [core] + lines + [plane]]
    return streams[: max(1, min(2, rows // (8 * math.prod(sizes.values()))))]


def body(inputs, weight, cotangent):
    in_ch, cells_x, cells_y, cells_z = inputs.shape
    out_ch = weight.shape[4]
    cells = inputs.transpose(1, 2, 0, 3)
    grads = cotangent.transpose(4, 5, 0, 1, 2, 3, 6).reshape(
        (cells_x, cells_y, 4, 2 * out_ch, cells_z)
    )
    taps = weight.transpose(0, 1, 2, 4, 3)
    vmem = pl.BlockSpec(memory_space=pltpu.VMEM)
    all_cells = (
        cells_x
        * lax.axis_size("gx")
        * cells_y
        * lax.axis_size("gy")
        * cells_z
        * lax.axis_size("gz")
    )
    rows = 32 * out_ch
    plan = reduce_plan(rows)
    exchanged = sum((1 << len(stage)) - 1 for stage in plan[0])
    copies = 22 + 2 * len(plan) * exchanged
    up, ig, total = pl.pallas_call(
        functools.partial(fused_kernel, plan, 1.0 / math.sqrt(all_cells)),
        out_shape=(
            jax.ShapeDtypeStruct((cells_x, cells_y, 4, 2 * out_ch, cells_z), jnp.bfloat16),
            jax.ShapeDtypeStruct((cells_x, cells_y, in_ch, cells_z), jnp.bfloat16),
            jax.ShapeDtypeStruct((4, 4, 4, out_ch, in_ch), jnp.float32),
        ),
        in_specs=[vmem] * 3,
        out_specs=[vmem] * 3,
        scratch_shapes=[
            pltpu.VMEM((cells_x + 2, cells_y + 2, in_ch, cells_z), jnp.bfloat16),
            pltpu.VMEM((cells_x + 1, cells_y + 1, 4, 2 * out_ch, cells_z), jnp.bfloat16),
            pltpu.VMEM((2, in_ch, 128), jnp.bfloat16),
            pltpu.VMEM((2, 4 * out_ch, 128), jnp.bfloat16),
            pltpu.VMEM((in_ch, 128), jnp.float32),
            pltpu.VMEM((4 * out_ch, 128), jnp.float32),
            pltpu.VMEM((in_ch, 128), jnp.bfloat16),
            pltpu.VMEM((4 * out_ch, 128), jnp.bfloat16),
            pltpu.VMEM((4, 4 * out_ch, 4 * in_ch), jnp.bfloat16),
            pltpu.VMEM((2, 2 * in_ch, 16 * out_ch), jnp.bfloat16),
            pltpu.VMEM((rows, 2 * in_ch), jnp.float32),
            pltpu.VMEM((rows, 2 * in_ch), jnp.float32),
            pltpu.VMEM((rows, 2 * in_ch), jnp.float32),
            pltpu.SemaphoreType.DMA((copies,)),
            pltpu.SemaphoreType.DMA((copies,)),
        ],
        compiler_params=pltpu.CompilerParams(
            collective_id=0, has_side_effects=True, vmem_limit_bytes=48 * 1024 * 1024
        ),
    )(cells, grads, taps)
    up = up.reshape((cells_x, cells_y, 2, 2, 2, out_ch, cells_z)).transpose(2, 3, 4, 5, 0, 1, 6)
    return up, ig.transpose(2, 0, 1, 3), total.transpose(0, 1, 2, 4, 3)


def solution(mesh):
    placed = (P(None, "gx", "gy", "gz"), P(), P(None, None, None, None, "gx", "gy", "gz"))
    return jax.shard_map(
        body,
        mesh=mesh,
        in_specs=placed,
        out_specs=(P(None, None, None, None, "gx", "gy", "gz"), P(None, "gx", "gy", "gz"), P()),
        check_vma=False,
    )
```

```python
import functools
import math

import jax
import jax.numpy as jnp
from jax import lax
from jax.experimental import pallas as pl
from jax.experimental.pallas import tpu as pltpu
from jax.sharding import PartitionSpec as P

TAPS = ((1, 3), (2, 0))
G_OFF = ((0, 1), (1, 0))
IN_SHIFT = ((0, -1), (0, 1))
PAIRS = [(p, h) for p in (0, 1) for h in (0, 1)]


MESH = pl.DeviceIdType.MESH


def dot(a, b):
    return jnp.dot(a, b, preferred_element_type=jnp.float32)


def dot_nt(a, b):
    return lax.dot_general(a, b, (((1,), (1,)), ((), ())), preferred_element_type=jnp.float32)


def fused_kernel(
    streams,
    factor,
    in_ref,
    g_ref,
    w_ref,
    up_ref,
    ig_ref,
    out_ref,
    ext_ref,
    gext_ref,
    zin_ref,
    zg_ref,
    pack_in,
    pack_g,
    face_in,
    face_g,
    wf_ref,
    wi_ref,
    total,
    landed,
    gathered,
    send_sem,
    recv_sem,
):
    cells_x, cells_y, in_ch, cells_z = in_ref.shape
    out_ch = g_ref.shape[3] // 2
    wide = zin_ref.shape[-1]
    row = cells_y + 2
    count_x, count_y = lax.axis_size("gx"), lax.axis_size("gy")
    me_x, me_y, me_z = lax.axis_index("gx"), lax.axis_index("gy"), lax.axis_index("gz")
    to_x = (lax.rem(me_x + count_x - 1, count_x), lax.rem(me_x + 1, count_x))
    to_y = (lax.rem(me_y + count_y - 1, count_y), lax.rem(me_y + 1, count_y))
    other_z = {"gz": 1 - me_z}

    groups = {}
    for stage in streams[0]:
        sides = [lax.rem(lax.div(lax.axis_index(axis), bit), 2) for axis, bit in stage]
        own = sum(side << i for i, side in enumerate(sides))
        partners = []
        for change in range(1, 1 << len(stage)):
            device, number = {}, own
            for i, (axis, bit) in enumerate(stage):
                if (change >> i) % 2:
                    step = 1 - 2 * sides[i]
                    device[axis] = device.get(axis, lax.axis_index(axis)) + bit * step
                    number = number + (step << i)
            partners.append((device, number))
        groups[stage] = (own, partners)

    greeted = [{"gx": x} for x in to_x] + [{"gy": y} for y in to_y]
    greeted += [{"gx": x, "gy": y} for x in to_x for y in to_y] + [other_z]
    greeted += [device for _, partners in groups.values() for device, _ in partners]
    barrier = pltpu.get_barrier_semaphore()
    for device in greeted:
        pl.semaphore_signal(barrier, inc=1, device_id=device, device_id_type=MESH)
    pl.semaphore_wait(barrier, len(greeted))

    used = [0]

    def send(src, dst, device):
        n = used[0]
        used[0] += 1
        copy = pltpu.make_async_remote_copy(
            src_ref=src,
            dst_ref=dst,
            send_sem=send_sem.at[n],
            recv_sem=recv_sem.at[n],
            device_id=device,
            device_id_type=MESH,
        )
        copy.start()
        return copy

    inner_x, inner_y = pl.ds(1, cells_x), pl.ds(1, cells_y)
    edge_x, edge_y = (0, cells_x - 1), (0, cells_y - 1)
    spot_x, spot_y = (cells_x + 1, 0), (cells_y + 1, 0)
    over_in = []
    for i in (0, 1):
        over_in.append(
            send(in_ref.at[edge_x[i]], ext_ref.at[spot_x[i], inner_y], {"gx": to_x[i]})
        )
        over_in.append(
            send(in_ref.at[:, edge_y[i]], ext_ref.at[inner_x, spot_y[i]], {"gy": to_y[i]})
        )
        for j in (0, 1):
            over_in.append(
                send(
                    in_ref.at[edge_x[i], edge_y[j]],
                    ext_ref.at[spot_x[i], spot_y[j]],
                    {"gx": to_x[i], "gy": to_y[j]},
                )
            )
    ext_ref[1 : cells_x + 1, 1 : cells_y + 1] = in_ref[...]
    for px in (0, 1):
        for py in (0, 1):
            n = px * 2 + py
            gext_ref[px : px + cells_x, py : py + cells_y, n] = g_ref[:, :, n]
    zin_ref[me_z] = jnp.zeros_like(zin_ref[0])
    zg_ref[1 - me_z] = jnp.zeros_like(zg_ref[0])

    source = (1 - me_z) * (cells_z - 1)
    half = pl.ds(pl.multiple_of((1 - me_z) * out_ch, out_ch), out_ch)

    def pack(dst, load, spots, stride):
        lane = lax.broadcasted_iota(jnp.int32, dst.shape, 1)
        held = dst[...]
        for x, y in spots:
            spot = x * stride + y
            value = load(x, y).astype(jnp.float32)
            turned = pltpu.roll(value, lax.rem(spot + wide - source, wide), 1)
            held = jnp.where(lane == spot, turned, held)
        dst[...] = held

    def load_in(x, y):
        return ext_ref[x, y]

    def load_g(x, y):
        return gext_ref[x, y, :, half, :].reshape((4 * out_ch, cells_z))

    inside = [(x, y) for x in range(1, cells_x + 1) for y in range(1, cells_y + 1)]
    around = [
        (x, y) for x in range(cells_x + 2) for y in range(cells_y + 2) if (x, y) not in inside
    ]
    inside_g = [(x, y) for x in range(1, cells_x) for y in range(1, cells_y)]
    around_g = [
        (x, y) for x in range(cells_x + 1) for y in range(cells_y + 1) if (x, y) not in inside_g
    ]
    pack_in[...] = jnp.zeros_like(pack_in)
    pack_g[...] = jnp.zeros_like(pack_g)
    pack(pack_in, load_in, inside, row)

    far_x, far_y = (cells_x, 0), (cells_y, 0)
    over_g = []
    for px in (0, 1):
        for py in (0, 1):
            n = px * 2 + py
            own_x, own_y = pl.ds(px, cells_x), pl.ds(py, cells_y)
            over_g.append(
                send(
                    g_ref.at[edge_x[px], :, n],
                    gext_ref.at[far_x[px], own_y, n],
                    {"gx": to_x[px]},
                )
            )
            over_g.append(
                send(
                    g_ref.at[:, edge_y[py], n],
                    gext_ref.at[own_x, far_y[py], n],
                    {"gy": to_y[py]},
                )
            )
            over_g.append(
                send(
                    g_ref.at[edge_x[px], edge_y[py], n],
                    gext_ref.at[far_x[px], far_y[py], n],
                    {"gx": to_x[px], "gy": to_y[py]},
                )
            )

    for px in (0, 1):
        for py in (0, 1):
            for pz, hz in PAIRS:
                wf_ref[px * 2 + py, pl.ds((2 * pz + hz) * out_ch, out_ch), :] = jnp.concatenate(
                    [
                        w_ref[TAPS[px][hx], TAPS[py][hy], TAPS[pz][hz]]
                        for hx in (0, 1)
                        for hy in (0, 1)
                    ],
                    axis=1,
                )
    for pz in (0, 1):
        rows = [
            jnp.concatenate(
                [w_ref[TAPS[px][hx], TAPS[py][hy], TAPS[pz][hz]] for hz in (0, 1)], axis=1
            )
            for px, hx in PAIRS
            for py, hy in PAIRS
        ]
        stacked = jnp.concatenate(rows, axis=0).astype(jnp.float32)
        wi_ref[pz] = stacked.T.astype(jnp.bfloat16)
    pack(pack_g, load_g, inside_g, row - 1)

    for copy in over_in:
        copy.wait()
    pack(pack_in, load_in, around, row)
    face_in[...] = pack_in[...].astype(jnp.bfloat16)
    over_z_in = send(face_in, zin_ref.at[me_z], other_z)

    lane = lax.broadcasted_iota(jnp.int32, (in_ch, cells_z), 1)
    first = lane == 0
    last = lane == cells_z - 1

    def rolled(value, amount):
        return pltpu.roll(value, amount % value.shape[-1], 1)

    over_z_in.wait()

    for px in (0, 1):
        for py in (0, 1):
            n = px * 2 + py
            edges = []
            for pz in (0, 1):
                packed = zin_ref[pz].astype(jnp.float32)
                rows = []
                for hx in (0, 1):
                    for hy in (0, 1):
                        spot = (1 + IN_SHIFT[px][hx]) * row + 1 + IN_SHIFT[py][hy]
                        rows.append(rolled(packed, -spot))
                stacked = jnp.concatenate(rows, axis=0).astype(jnp.bfloat16)
                edges.append(dot(wf_ref[n, pl.ds((2 * pz + 1) * out_ch, out_ch), :], stacked))
            for x in range(cells_x):
                rows = []
                for hx in (0, 1):
                    for hy in (0, 1):
                        rows.append(
                            jnp.concatenate(
                                [
                                    ext_ref[x + 1 + IN_SHIFT[px][hx], y + 1 + IN_SHIFT[py][hy]]
                                    for y in range(cells_y)
                                ],
                                axis=1,
                            )
                        )
                product = dot(wf_ref[n], jnp.concatenate(rows, axis=0))
                for y in range(cells_y):
                    cols = slice(y * cells_z, (y + 1) * cells_z)
                    spot = x * row + y
                    even = product[:out_ch, cols] + jnp.where(
                        first[:out_ch],
                        rolled(edges[0], -spot),
                        rolled(product[out_ch : 2 * out_ch, cols], 1),
                    )
                    odd = product[2 * out_ch : 3 * out_ch, cols] + jnp.where(
                        last[:out_ch],
                        rolled(edges[1], cells_z - 1 - spot),
                        rolled(product[3 * out_ch :, cols], -1),
                    )
                    up_ref[x, y, n, :out_ch] = even.astype(jnp.bfloat16)
                    up_ref[x, y, n, out_ch:] = odd.astype(jnp.bfloat16)

    for copy in over_g:
        copy.wait()

    def gradients(x, pz):
        rows = []
        for px, hx in PAIRS:
            for py, hy in PAIRS:
                rows.append(
                    jnp.concatenate(
                        [
                            gext_ref[
                                x + G_OFF[px][hx],
                                y + G_OFF[py][hy],
                                px * 2 + py,
                                pl.ds(pz * out_ch, out_ch),
                                :,
                            ]
                            for y in range(cells_y)
                        ],
                        axis=1,
                    )
                )
        return jnp.concatenate(rows, axis=0)

    each = total.shape[0] // len(streams)
    begin = [j * each for j in range(len(streams))]
    length = [each for _ in streams]
    filled = [j * each for j in range(len(streams))]
    kept = [[] for _ in streams]
    flying = [None for _ in streams]

    def scatter(j, stage):
        own, partners = groups[stage]
        size = length[j] // (len(partners) + 1)
        copies = []
        for device, number in partners:
            give = pl.multiple_of(begin[j] + number * size, 8)
            area = pl.ds(filled[j], size)
            filled[j] += size
            copies.append((send(total.at[pl.ds(give, size)], landed.at[area], device), area))
        begin[j] = pl.multiple_of(begin[j] + own * size, 8)
        length[j] = size
        kept[j].append(begin[j])
        flying[j] = copies

    def settle(j):
        mine = pl.ds(begin[j], length[j])
        value = total[mine, :]
        for copy, area in flying[j]:
            copy.wait()
            value = value + landed[area, :]
        total[mine, :] = value

    def gather(j, depth):
        size = length[j]
        mine = pl.ds(kept[j][depth], size)
        flying[j] = [
            send(gathered.at[mine], gathered.at[mine], device)
            for device, _ in groups[streams[j][depth]][1]
        ]
        length[j] = size * (len(flying[j]) + 1)

    def arrive(j):
        for copy in flying[j]:
            copy.wait()

    half_rows = 16 * out_ch
    for pz in (0, 1):
        packed = zin_ref[pz].astype(jnp.float32)
        for x in range(cells_x):
            shifted = []
            for y in range(cells_y):
                here = ext_ref[x + 1, y + 1]
                spot = (x + 1) * row + y + 1
                if pz == 0:
                    near = jnp.where(
                        first, rolled(packed, -spot), rolled(here.astype(jnp.float32), 1)
                    )
                else:
                    near = jnp.where(
                        last,
                        rolled(packed, cells_z - 1 - spot),
                        rolled(here.astype(jnp.float32), -1),
                    )
                shifted.append(jnp.concatenate([here, near.astype(jnp.bfloat16)], axis=0))
            part = dot_nt(gradients(x, pz), jnp.concatenate(shifted, axis=1))
            spots = pl.ds(pz * half_rows, half_rows)
            total[spots, :] = part if x == 0 else total[spots, :] + part
        if len(streams) == 2:
            scatter(pz, streams[pz][0])
    if len(streams) == 1:
        scatter(0, streams[0][0])

    pack(pack_g, load_g, around_g, row - 1)
    face_g[...] = pack_g[...].astype(jnp.bfloat16)
    over_z_g = send(face_g, zg_ref.at[1 - me_z], other_z)

    stages = len(streams[0])
    everyone = range(len(streams))

    def advance(depth):
        for j in everyone:
            settle(j)
            scatter(j, streams[j][depth])

    advance(1)
    over_z_g.wait()
    edge_ig = []
    for pz in (0, 1):
        rows = []
        for px, hx in PAIRS:
            for py, hy in PAIRS:
                packed = zg_ref[pz, pl.ds((px * 2 + py) * out_ch, out_ch), :].astype(jnp.float32)
                rows.append(rolled(packed, -(G_OFF[px][hx] * (row - 1) + G_OFF[py][hy])))
        stacked = jnp.concatenate(rows, axis=0).astype(jnp.bfloat16)
        edge_ig.append(dot(wi_ref[pz, in_ch : 2 * in_ch, :], stacked))

    def input_row(x):
        parts = [[], []]
        for pz in (0, 1):
            product = dot(wi_ref[pz], gradients(x, pz))
            for y in range(cells_y):
                cols = slice(y * cells_z, (y + 1) * cells_z)
                spot = x * (row - 1) + y
                if pz == 0:
                    far = jnp.where(
                        last,
                        rolled(edge_ig[0], cells_z - 1 - spot),
                        rolled(product[in_ch:, cols], -1),
                    )
                else:
                    far = jnp.where(
                        first, rolled(edge_ig[1], -spot), rolled(product[in_ch:, cols], 1)
                    )
                parts[pz].append(product[:in_ch, cols] + far)
        for y in range(cells_y):
            ig_ref[x, y] = (parts[0][y] + parts[1][y]).astype(jnp.bfloat16)

    left = list(range(cells_x))

    def compute_some():
        if left:
            input_row(left.pop(0))

    for depth in range(2, stages):
        compute_some()
        advance(depth)
    compute_some()
    for j in everyone:
        settle(j)
        mine = pl.ds(begin[j], length[j])
        gathered[mine, :] = total[mine, :]
        gather(j, stages - 1)
    for depth in reversed(range(stages - 1)):
        compute_some()
        for j in everyone:
            arrive(j)
            gather(j, depth)
    while left:
        compute_some()
    for j in everyone:
        arrive(j)
        for pz in (0, 1):
            if len(streams) == 2 and pz != j:
                continue
            for a, (px, hx) in enumerate(PAIRS):
                for b, (py, hy) in enumerate(PAIRS):
                    spots = pl.ds(((pz * 4 + a) * 4 + b) * out_ch, out_ch)
                    block = gathered[spots, :] * factor
                    for hz in (0, 1):
                        out_ref[TAPS[px][hx], TAPS[py][hy], TAPS[pz][hz]] = block[
                            :, hz * in_ch : (hz + 1) * in_ch
                        ]


def reduce_plan(rows):
    sizes = {axis: lax.axis_size(axis) for axis in ("gz", "gx", "gy")}
    bits = {
        axis: [(axis, 1 << bit) for bit in range(size.bit_length() - 1)]
        for axis, size in sizes.items()
    }
    plane = tuple(bits["gz"] + bits["gx"][1:])
    lines = [tuple(bits["gy"][i : i + 2]) for i in range(0, len(bits["gy"]), 2)]
    core = tuple(bits["gx"][:1])
    streams = [[core, plane] + lines, [core] + lines + [plane]]
    return streams[: max(1, min(2, rows // (8 * math.prod(sizes.values()))))]


def body(inputs, weight, cotangent):
    in_ch, cells_x, cells_y, cells_z = inputs.shape
    out_ch = weight.shape[4]
    cells = inputs.transpose(1, 2, 0, 3)
    grads = cotangent.transpose(4, 5, 0, 1, 2, 3, 6).reshape(
        (cells_x, cells_y, 4, 2 * out_ch, cells_z)
    )
    taps = weight.transpose(0, 1, 2, 4, 3)
    vmem = pl.BlockSpec(memory_space=pltpu.VMEM)
    all_cells = (
        cells_x
        * lax.axis_size("gx")
        * cells_y
        * lax.axis_size("gy")
        * cells_z
        * lax.axis_size("gz")
    )
    rows = 32 * out_ch
    plan = reduce_plan(rows)
    exchanged = sum((1 << len(stage)) - 1 for stage in plan[0])
    copies = 22 + 2 * len(plan) * exchanged
    up, ig, total = pl.pallas_call(
        functools.partial(fused_kernel, plan, 1.0 / math.sqrt(all_cells)),
        out_shape=(
            jax.ShapeDtypeStruct((cells_x, cells_y, 4, 2 * out_ch, cells_z), jnp.bfloat16),
            jax.ShapeDtypeStruct((cells_x, cells_y, in_ch, cells_z), jnp.bfloat16),
            jax.ShapeDtypeStruct((4, 4, 4, out_ch, in_ch), jnp.float32),
        ),
        in_specs=[vmem] * 3,
        out_specs=[vmem] * 3,
        scratch_shapes=[
            pltpu.VMEM((cells_x + 2, cells_y + 2, in_ch, cells_z), jnp.bfloat16),
            pltpu.VMEM((cells_x + 1, cells_y + 1, 4, 2 * out_ch, cells_z), jnp.bfloat16),
            pltpu.VMEM((2, in_ch, 128), jnp.bfloat16),
            pltpu.VMEM((2, 4 * out_ch, 128), jnp.bfloat16),
            pltpu.VMEM((in_ch, 128), jnp.float32),
            pltpu.VMEM((4 * out_ch, 128), jnp.float32),
            pltpu.VMEM((in_ch, 128), jnp.bfloat16),
            pltpu.VMEM((4 * out_ch, 128), jnp.bfloat16),
            pltpu.VMEM((4, 4 * out_ch, 4 * in_ch), jnp.bfloat16),
            pltpu.VMEM((2, 2 * in_ch, 16 * out_ch), jnp.bfloat16),
            pltpu.VMEM((rows, 2 * in_ch), jnp.float32),
            pltpu.VMEM((rows, 2 * in_ch), jnp.float32),
            pltpu.VMEM((rows, 2 * in_ch), jnp.float32),
            pltpu.SemaphoreType.DMA((copies,)),
            pltpu.SemaphoreType.DMA((copies,)),
        ],
        compiler_params=pltpu.CompilerParams(
            collective_id=0, has_side_effects=True, vmem_limit_bytes=24 * 1024 * 1024
        ),
    )(cells, grads, taps)
    up = up.reshape((cells_x, cells_y, 2, 2, 2, out_ch, cells_z)).transpose(2, 3, 4, 5, 0, 1, 6)
    return up, ig.transpose(2, 0, 1, 3), total.transpose(0, 1, 2, 4, 3)


def solution(mesh):
    placed = (P(None, "gx", "gy", "gz"), P(), P(None, None, None, None, "gx", "gy", "gz"))
    return jax.shard_map(
        body,
        mesh=mesh,
        in_specs=placed,
        out_specs=(P(None, None, None, None, "gx", "gy", "gz"), P(None, "gx", "gy", "gz"), P()),
        check_vma=False,
    )
```

```python
import functools
import math

import jax
import jax.numpy as jnp
from jax import lax
from jax.experimental import pallas as pl
from jax.experimental.pallas import tpu as pltpu
from jax.sharding import PartitionSpec as P

TAPS = ((1, 3), (2, 0))
G_OFF = ((0, 1), (1, 0))
IN_SHIFT = ((0, -1), (0, 1))
PAIRS = [(p, h) for p in (0, 1) for h in (0, 1)]


MESH = pl.DeviceIdType.MESH


def dot(a, b):
    return jnp.dot(a, b, preferred_element_type=jnp.float32)


def dot_nt(a, b):
    return lax.dot_general(a, b, (((1,), (1,)), ((), ())), preferred_element_type=jnp.float32)


def fused_kernel(
    streams,
    factor,
    in_ref,
    g_ref,
    w_ref,
    up_ref,
    ig_ref,
    out_ref,
    cell_up,
    ext_ref,
    gext_ref,
    zin_ref,
    zg_ref,
    pack_in,
    pack_g,
    face_in,
    face_g,
    wf_ref,
    wi_ref,
    total,
    landed,
    gathered,
    send_sem,
    recv_sem,
):
    cells_x, cells_y, in_ch, cells_z = in_ref.shape
    out_ch = g_ref.shape[3] // 2
    wide = zin_ref.shape[-1]
    row = cells_y + 2
    count_x, count_y = lax.axis_size("gx"), lax.axis_size("gy")
    me_x, me_y, me_z = lax.axis_index("gx"), lax.axis_index("gy"), lax.axis_index("gz")
    to_x = (lax.rem(me_x + count_x - 1, count_x), lax.rem(me_x + 1, count_x))
    to_y = (lax.rem(me_y + count_y - 1, count_y), lax.rem(me_y + 1, count_y))
    other_z = {"gz": 1 - me_z}

    groups = {}
    for stage in streams[0]:
        sides = [lax.rem(lax.div(lax.axis_index(axis), bit), 2) for axis, bit in stage]
        own = sum(side << i for i, side in enumerate(sides))
        partners = []
        for change in range(1, 1 << len(stage)):
            device, number = {}, own
            for i, (axis, bit) in enumerate(stage):
                if (change >> i) % 2:
                    step = 1 - 2 * sides[i]
                    device[axis] = device.get(axis, lax.axis_index(axis)) + bit * step
                    number = number + (step << i)
            partners.append((device, number))
        groups[stage] = (own, partners)

    greeted = [{"gx": x} for x in to_x] + [{"gy": y} for y in to_y]
    greeted += [{"gx": x, "gy": y} for x in to_x for y in to_y] + [other_z]
    greeted += [device for _, partners in groups.values() for device, _ in partners]
    barrier = pltpu.get_barrier_semaphore()
    for device in greeted:
        pl.semaphore_signal(barrier, inc=1, device_id=device, device_id_type=MESH)
    pl.semaphore_wait(barrier, len(greeted))

    used = [0]

    def send(src, dst, device):
        n = used[0]
        used[0] += 1
        copy = pltpu.make_async_remote_copy(
            src_ref=src,
            dst_ref=dst,
            send_sem=send_sem.at[n],
            recv_sem=recv_sem.at[n],
            device_id=device,
            device_id_type=MESH,
        )
        copy.start()
        return copy

    inner_x, inner_y = pl.ds(1, cells_x), pl.ds(1, cells_y)
    edge_x, edge_y = (0, cells_x - 1), (0, cells_y - 1)
    spot_x, spot_y = (cells_x + 1, 0), (cells_y + 1, 0)
    over_in = []
    for i in (0, 1):
        over_in.append(
            send(in_ref.at[edge_x[i]], ext_ref.at[spot_x[i], inner_y], {"gx": to_x[i]})
        )
        over_in.append(
            send(in_ref.at[:, edge_y[i]], ext_ref.at[inner_x, spot_y[i]], {"gy": to_y[i]})
        )
        for j in (0, 1):
            over_in.append(
                send(
                    in_ref.at[edge_x[i], edge_y[j]],
                    ext_ref.at[spot_x[i], spot_y[j]],
                    {"gx": to_x[i], "gy": to_y[j]},
                )
            )
    ext_ref[1 : cells_x + 1, 1 : cells_y + 1] = in_ref[...]
    for px in (0, 1):
        for py in (0, 1):
            n = px * 2 + py
            gext_ref[px : px + cells_x, py : py + cells_y, n] = g_ref[:, :, n]
    zin_ref[me_z] = jnp.zeros_like(zin_ref[0])
    zg_ref[1 - me_z] = jnp.zeros_like(zg_ref[0])

    source = (1 - me_z) * (cells_z - 1)
    half = pl.ds(pl.multiple_of((1 - me_z) * out_ch, out_ch), out_ch)

    def pack(dst, load, spots, stride):
        lane = lax.broadcasted_iota(jnp.int32, dst.shape, 1)
        held = dst[...]
        for x, y in spots:
            spot = x * stride + y
            value = load(x, y).astype(jnp.float32)
            turned = pltpu.roll(value, lax.rem(spot + wide - source, wide), 1)
            held = jnp.where(lane == spot, turned, held)
        dst[...] = held

    def load_in(x, y):
        return ext_ref[x, y]

    def load_g(x, y):
        return gext_ref[x, y, :, half, :].reshape((4 * out_ch, cells_z))

    inside = [(x, y) for x in range(1, cells_x + 1) for y in range(1, cells_y + 1)]
    around = [
        (x, y) for x in range(cells_x + 2) for y in range(cells_y + 2) if (x, y) not in inside
    ]
    inside_g = [(x, y) for x in range(1, cells_x) for y in range(1, cells_y)]
    around_g = [
        (x, y) for x in range(cells_x + 1) for y in range(cells_y + 1) if (x, y) not in inside_g
    ]
    pack_in[...] = jnp.zeros_like(pack_in)
    pack_g[...] = jnp.zeros_like(pack_g)
    pack(pack_in, load_in, inside, row)

    far_x, far_y = (cells_x, 0), (cells_y, 0)
    over_g = []
    for px in (0, 1):
        for py in (0, 1):
            n = px * 2 + py
            own_x, own_y = pl.ds(px, cells_x), pl.ds(py, cells_y)
            over_g.append(
                send(
                    g_ref.at[edge_x[px], :, n],
                    gext_ref.at[far_x[px], own_y, n],
                    {"gx": to_x[px]},
                )
            )
            over_g.append(
                send(
                    g_ref.at[:, edge_y[py], n],
                    gext_ref.at[own_x, far_y[py], n],
                    {"gy": to_y[py]},
                )
            )
            over_g.append(
                send(
                    g_ref.at[edge_x[px], edge_y[py], n],
                    gext_ref.at[far_x[px], far_y[py], n],
                    {"gx": to_x[px], "gy": to_y[py]},
                )
            )

    for px in (0, 1):
        for py in (0, 1):
            for pz, hz in PAIRS:
                wf_ref[px * 2 + py, pl.ds((2 * pz + hz) * out_ch, out_ch), :] = jnp.concatenate(
                    [
                        w_ref[TAPS[px][hx], TAPS[py][hy], TAPS[pz][hz]]
                        for hx in (0, 1)
                        for hy in (0, 1)
                    ],
                    axis=1,
                )
    for pz in (0, 1):
        rows = [
            jnp.concatenate(
                [w_ref[TAPS[px][hx], TAPS[py][hy], TAPS[pz][hz]] for hz in (0, 1)], axis=1
            )
            for px, hx in PAIRS
            for py, hy in PAIRS
        ]
        stacked = jnp.concatenate(rows, axis=0).astype(jnp.float32)
        wi_ref[pz] = stacked.T.astype(jnp.bfloat16)
    pack(pack_g, load_g, inside_g, row - 1)

    for copy in over_in:
        copy.wait()
    pack(pack_in, load_in, around, row)
    face_in[...] = pack_in[...].astype(jnp.bfloat16)
    over_z_in = send(face_in, zin_ref.at[me_z], other_z)

    lane = lax.broadcasted_iota(jnp.int32, (in_ch, cells_z), 1)
    first = lane == 0
    last = lane == cells_z - 1

    def rolled(value, amount):
        return pltpu.roll(value, amount % value.shape[-1], 1)

    over_z_in.wait()

    for px in (0, 1):
        for py in (0, 1):
            n = px * 2 + py
            edges = []
            for pz in (0, 1):
                packed = zin_ref[pz].astype(jnp.float32)
                rows = []
                for hx in (0, 1):
                    for hy in (0, 1):
                        spot = (1 + IN_SHIFT[px][hx]) * row + 1 + IN_SHIFT[py][hy]
                        rows.append(rolled(packed, -spot))
                stacked = jnp.concatenate(rows, axis=0).astype(jnp.bfloat16)
                edges.append(dot(wf_ref[n, pl.ds((2 * pz + 1) * out_ch, out_ch), :], stacked))
            for x in range(cells_x):
                rows = []
                for hx in (0, 1):
                    for hy in (0, 1):
                        rows.append(
                            jnp.concatenate(
                                [
                                    ext_ref[x + 1 + IN_SHIFT[px][hx], y + 1 + IN_SHIFT[py][hy]]
                                    for y in range(cells_y)
                                ],
                                axis=1,
                            )
                        )
                product = dot(wf_ref[n], jnp.concatenate(rows, axis=0))
                for y in range(cells_y):
                    cols = slice(y * cells_z, (y + 1) * cells_z)
                    spot = x * row + y
                    even = product[:out_ch, cols] + jnp.where(
                        first[:out_ch],
                        rolled(edges[0], -spot),
                        rolled(product[out_ch : 2 * out_ch, cols], 1),
                    )
                    odd = product[2 * out_ch : 3 * out_ch, cols] + jnp.where(
                        last[:out_ch],
                        rolled(edges[1], cells_z - 1 - spot),
                        rolled(product[3 * out_ch :, cols], -1),
                    )
                    cell_up[x, y, n, :out_ch] = even.astype(jnp.bfloat16)
                    cell_up[x, y, n, out_ch:] = odd.astype(jnp.bfloat16)

    for copy in over_g:
        copy.wait()

    def gradients(x, pz):
        rows = []
        for px, hx in PAIRS:
            for py, hy in PAIRS:
                rows.append(
                    jnp.concatenate(
                        [
                            gext_ref[
                                x + G_OFF[px][hx],
                                y + G_OFF[py][hy],
                                px * 2 + py,
                                pl.ds(pz * out_ch, out_ch),
                                :,
                            ]
                            for y in range(cells_y)
                        ],
                        axis=1,
                    )
                )
        return jnp.concatenate(rows, axis=0)

    each = total.shape[0] // len(streams)
    begin = [j * each for j in range(len(streams))]
    length = [each for _ in streams]
    filled = [j * each for j in range(len(streams))]
    kept = [[] for _ in streams]
    flying = [None for _ in streams]

    def scatter(j, stage):
        own, partners = groups[stage]
        size = length[j] // (len(partners) + 1)
        copies = []
        for device, number in partners:
            give = pl.multiple_of(begin[j] + number * size, 8)
            area = pl.ds(filled[j], size)
            filled[j] += size
            copies.append((send(total.at[pl.ds(give, size)], landed.at[area], device), area))
        begin[j] = pl.multiple_of(begin[j] + own * size, 8)
        length[j] = size
        kept[j].append(begin[j])
        flying[j] = copies

    def settle(j):
        mine = pl.ds(begin[j], length[j])
        value = total[mine, :]
        for copy, area in flying[j]:
            copy.wait()
            value = value + landed[area, :]
        total[mine, :] = value

    def gather(j, depth):
        size = length[j]
        mine = pl.ds(kept[j][depth], size)
        flying[j] = [
            send(gathered.at[mine], gathered.at[mine], device)
            for device, _ in groups[streams[j][depth]][1]
        ]
        length[j] = size * (len(flying[j]) + 1)

    def arrive(j):
        for copy in flying[j]:
            copy.wait()

    half_rows = 16 * out_ch
    for pz in (0, 1):
        packed = zin_ref[pz].astype(jnp.float32)
        for x in range(cells_x):
            shifted = []
            for y in range(cells_y):
                here = ext_ref[x + 1, y + 1]
                spot = (x + 1) * row + y + 1
                if pz == 0:
                    near = jnp.where(
                        first, rolled(packed, -spot), rolled(here.astype(jnp.float32), 1)
                    )
                else:
                    near = jnp.where(
                        last,
                        rolled(packed, cells_z - 1 - spot),
                        rolled(here.astype(jnp.float32), -1),
                    )
                shifted.append(jnp.concatenate([here, near.astype(jnp.bfloat16)], axis=0))
            part = dot_nt(gradients(x, pz), jnp.concatenate(shifted, axis=1))
            spots = pl.ds(pz * half_rows, half_rows)
            total[spots, :] = part if x == 0 else total[spots, :] + part
        if len(streams) == 2:
            scatter(pz, streams[pz][0])
    if len(streams) == 1:
        scatter(0, streams[0][0])

    pack(pack_g, load_g, around_g, row - 1)
    face_g[...] = pack_g[...].astype(jnp.bfloat16)
    over_z_g = send(face_g, zg_ref.at[1 - me_z], other_z)

    stages = len(streams[0])
    everyone = range(len(streams))

    def advance(depth):
        for j in everyone:
            settle(j)
            scatter(j, streams[j][depth])

    advance(1)
    over_z_g.wait()
    edge_ig = []
    for pz in (0, 1):
        rows = []
        for px, hx in PAIRS:
            for py, hy in PAIRS:
                packed = zg_ref[pz, pl.ds((px * 2 + py) * out_ch, out_ch), :].astype(jnp.float32)
                rows.append(rolled(packed, -(G_OFF[px][hx] * (row - 1) + G_OFF[py][hy])))
        stacked = jnp.concatenate(rows, axis=0).astype(jnp.bfloat16)
        edge_ig.append(dot(wi_ref[pz, in_ch : 2 * in_ch, :], stacked))

    def input_row(x):
        parts = [[], []]
        for pz in (0, 1):
            product = dot(wi_ref[pz], gradients(x, pz))
            for y in range(cells_y):
                cols = slice(y * cells_z, (y + 1) * cells_z)
                spot = x * (row - 1) + y
                if pz == 0:
                    far = jnp.where(
                        last,
                        rolled(edge_ig[0], cells_z - 1 - spot),
                        rolled(product[in_ch:, cols], -1),
                    )
                else:
                    far = jnp.where(
                        first, rolled(edge_ig[1], -spot), rolled(product[in_ch:, cols], 1)
                    )
                parts[pz].append(product[:in_ch, cols] + far)
        ig_ref[:, x] = jnp.stack(
            [parts[0][y] + parts[1][y] for y in range(cells_y)], axis=1
        ).astype(jnp.bfloat16)

    def relay_up(x):
        for n in range(4):
            for pz in (0, 1):
                tiles = [
                    cell_up[x, y, n, pl.ds(pz * out_ch, out_ch), :].astype(jnp.float32)
                    for y in range(cells_y)
                ]
                up_ref[n // 2, n % 2, pz, :, x] = jnp.stack(tiles, axis=1).astype(jnp.bfloat16)

    left = [functools.partial(input_row, x) for x in range(cells_x)]
    left += [functools.partial(relay_up, x) for x in range(cells_x)]

    def compute_some():
        for _ in range(2):
            if left:
                left.pop(0)()

    for depth in range(2, stages):
        compute_some()
        advance(depth)
    compute_some()
    for j in everyone:
        settle(j)
        mine = pl.ds(begin[j], length[j])
        gathered[mine, :] = total[mine, :]
        gather(j, stages - 1)
    for depth in reversed(range(stages - 1)):
        compute_some()
        for j in everyone:
            arrive(j)
            gather(j, depth)
    while left:
        compute_some()
    for j in everyone:
        arrive(j)
        for pz in (0, 1):
            if len(streams) == 2 and pz != j:
                continue
            for a, (px, hx) in enumerate(PAIRS):
                for b, (py, hy) in enumerate(PAIRS):
                    spots = pl.ds(((pz * 4 + a) * 4 + b) * out_ch, out_ch)
                    block = gathered[spots, :] * factor
                    for hz in (0, 1):
                        out_ref[TAPS[px][hx], TAPS[py][hy], TAPS[pz][hz]] = block[
                            :, hz * in_ch : (hz + 1) * in_ch
                        ]


def reduce_plan(rows):
    sizes = {axis: lax.axis_size(axis) for axis in ("gz", "gx", "gy")}
    bits = {
        axis: [(axis, 1 << bit) for bit in range(size.bit_length() - 1)]
        for axis, size in sizes.items()
    }
    plane = tuple(bits["gz"] + bits["gx"][1:])
    lines = [tuple(bits["gy"][i : i + 2]) for i in range(0, len(bits["gy"]), 2)]
    core = tuple(bits["gx"][:1])
    streams = [[core, plane] + lines, [core] + lines + [plane]]
    return streams[: max(1, min(2, rows // (8 * math.prod(sizes.values()))))]


def body(inputs, weight, cotangent):
    in_ch, cells_x, cells_y, cells_z = inputs.shape
    out_ch = weight.shape[4]
    cells = inputs.transpose(1, 2, 0, 3)
    grads = cotangent.transpose(4, 5, 0, 1, 2, 3, 6).reshape(
        (cells_x, cells_y, 4, 2 * out_ch, cells_z)
    )
    taps = weight.transpose(0, 1, 2, 4, 3)
    vmem = pl.BlockSpec(memory_space=pltpu.VMEM)
    all_cells = (
        cells_x
        * lax.axis_size("gx")
        * cells_y
        * lax.axis_size("gy")
        * cells_z
        * lax.axis_size("gz")
    )
    rows = 32 * out_ch
    plan = reduce_plan(rows)
    exchanged = sum((1 << len(stage)) - 1 for stage in plan[0])
    copies = 22 + 2 * len(plan) * exchanged
    up, ig, total = pl.pallas_call(
        functools.partial(fused_kernel, plan, 1.0 / math.sqrt(all_cells)),
        out_shape=(
            jax.ShapeDtypeStruct(cotangent.shape, jnp.bfloat16),
            jax.ShapeDtypeStruct(inputs.shape, jnp.bfloat16),
            jax.ShapeDtypeStruct((4, 4, 4, out_ch, in_ch), jnp.float32),
        ),
        in_specs=[vmem] * 3,
        out_specs=[vmem] * 3,
        scratch_shapes=[
            pltpu.VMEM((cells_x, cells_y, 4, 2 * out_ch, cells_z), jnp.bfloat16),
            pltpu.VMEM((cells_x + 2, cells_y + 2, in_ch, cells_z), jnp.bfloat16),
            pltpu.VMEM((cells_x + 1, cells_y + 1, 4, 2 * out_ch, cells_z), jnp.bfloat16),
            pltpu.VMEM((2, in_ch, 128), jnp.bfloat16),
            pltpu.VMEM((2, 4 * out_ch, 128), jnp.bfloat16),
            pltpu.VMEM((in_ch, 128), jnp.float32),
            pltpu.VMEM((4 * out_ch, 128), jnp.float32),
            pltpu.VMEM((in_ch, 128), jnp.bfloat16),
            pltpu.VMEM((4 * out_ch, 128), jnp.bfloat16),
            pltpu.VMEM((4, 4 * out_ch, 4 * in_ch), jnp.bfloat16),
            pltpu.VMEM((2, 2 * in_ch, 16 * out_ch), jnp.bfloat16),
            pltpu.VMEM((rows, 2 * in_ch), jnp.float32),
            pltpu.VMEM((rows, 2 * in_ch), jnp.float32),
            pltpu.VMEM((rows, 2 * in_ch), jnp.float32),
            pltpu.SemaphoreType.DMA((copies,)),
            pltpu.SemaphoreType.DMA((copies,)),
        ],
        compiler_params=pltpu.CompilerParams(
            collective_id=0, has_side_effects=True, vmem_limit_bytes=24 * 1024 * 1024
        ),
    )(cells, grads, taps)
    return up, ig, total.transpose(0, 1, 2, 4, 3)


def solution(mesh):
    placed = (P(None, "gx", "gy", "gz"), P(), P(None, None, None, None, "gx", "gy", "gz"))
    return jax.shard_map(
        body,
        mesh=mesh,
        in_specs=placed,
        out_specs=(P(None, None, None, None, "gx", "gy", "gz"), P(None, "gx", "gy", "gz"), P()),
        check_vma=False,
    )
```
